512 devices in a mesh: row: 256 (over z, y, x), col: 2 (over core).
Axes of the slice: x: 4, y: 8, z: 8, core: 2. Of those that a mesh axis runs over, the one named last changes fastest.
Arguments:
- leaf_basis: float32 [4096, 128, 64], P(('row', 'col')), may hold values from -0.5 to 0.5
- local_transfer: bfloat16 [7168, 64, 64], P(('row', 'col')), may hold values from -0.5 to 0.5
- col_transfer: bfloat16 [256, 2, 64, 64], P('row'), may hold values from -0.5 to 0.5
- row_transfer: bfloat16 [256, 8, 64, 64], P('row'), as said below
- coupling: bfloat16 [122880, 64, 64], P(('row', 'col')), may hold values from -6 to 6
- slot_block_row: int32 [122880], P(('row', 'col')), may hold values from 0 to 7, as said below
- block_col: int32 [122880], P(('row', 'col')), may hold values from 0 to 47, as said below
- block_valid: int32 [122880], P(('row', 'col')), may hold values from 0 to 1, as said below
Outputs:
- projected: bfloat16 [122880, 64, 64], P(('row', 'col'))
- path_factor: float32 [512, 9, 64, 64], P(('row', 'col'))
The draws below stay inside these ranges and needn't reach their ends.
Inputs may be any that keep to these rules, and one draw needn't show every extreme that they name: row_transfer[r, k] is the transfer of the ancestor k levels above row subtree r's cluster, so it is the same for all r with the same r // 2^k. `slot_block_row`: at each level, a device block's slots name each of its clusters of that level exactly 16 times. `block_col`: at each level, some slot of every device block names the first and some other slot the last of the listed clusters of that level. `block_valid`: at each level, a device block's real slots come first and are at least half of its slots of that level.
All inputs are finite; a program needn't handle non-finite values.
Results may differ from the reference program's by a relative error of at most 0.0015.
Values sent between devices are 32-bit elements; how exact they have to be, the bound alone decides.
A program may use at most 128 MiB of HBM per device.

```python
import jax
import jax.numpy as jnp
from jax import lax

LEAF = 128
BASIS_RANK = 64
LEAF_DEV = 8
NB = 16
NLEAF = 4096
NLOCAL = 7168
TOTAL_SLOTS = 122880
RLEV = 8
N_ROW = 256
N_COL = 2


def draw_row_transfer(key, part):
    source = jax.random.normal(key, (RLEV, N_ROW, BASIS_RANK, BASIS_RANK), jnp.float32) * (2 * BASIS_RANK) ** (-0.5)
    layers = []
    for height in range(RLEV):
        owners = jnp.arange(N_ROW) // 2 ** height
        layers.append(jnp.take(source[height], owners, axis=0))
    return jnp.stack(layers, axis=1).astype(jnp.bfloat16)


def draw_slot_block_row(key, part):
    devices_all = N_ROW * N_COL
    pieces = []
    for height in range(4):
        slots = NB * (LEAF_DEV // 2 ** height)
        key_list = jax.random.split(jax.random.fold_in(key, 101 + height), devices_all)

        def shuffle_one(single):
            return jax.random.permutation(single, slots)
        permuted_order = jax.vmap(shuffle_one)(key_list)
        pieces.append(permuted_order // NB)
    return jnp.concatenate(pieces, axis=1).reshape(-1).astype(jnp.int32)


def draw_block_col(key, part):
    devices_all = N_ROW * N_COL
    pieces = []
    for height in range(4):
        slots = NB * (LEAF_DEV // 2 ** height)
        limit = 3 * N_COL * (LEAF_DEV // 2 ** height)
        columns = jax.random.randint(jax.random.fold_in(key, 201 + height), (devices_all, slots), 0, limit)
        chosen = jax.random.randint(jax.random.fold_in(key, 301 + height), (devices_all, 1), 0, slots)
        positions = jnp.arange(slots)[None, :]
        columns = jnp.where(positions == chosen, limit - 1, columns)
        columns = jnp.where(positions == (chosen + 1) % slots, 0, columns)
        pieces.append(columns)
    return jnp.concatenate(pieces, axis=1).reshape(-1).astype(jnp.int32)


def draw_block_valid(key, part):
    devices_all = N_ROW * N_COL
    pieces = []
    for height in range(4):
        slots = NB * (LEAF_DEV // 2 ** height)
        filled = jax.random.randint(jax.random.fold_in(key, 401 + height), (devices_all, 1), (slots + 1) // 2, slots + 1)
        positions = jnp.arange(slots)[None, :]
        pieces.append((positions < filled).astype(jnp.int32))
    return jnp.concatenate(pieces, axis=1).reshape(-1).astype(jnp.int32)


def level_of(key, shape, cuts, low, high):
    level = 1.0
    for dim, shards_of in cuts:
        draws = jax.random.uniform(jax.random.fold_in(jax.random.fold_in(key, 6), dim), (shards_of,), jnp.float32, low / len(cuts), high / len(cuts))
        level = level * jnp.repeat(jnp.exp(draws), shape[dim] // shards_of).reshape((-1,) + (1,) * (len(shape) - 1 - dim))
    return level


def scatter_about(key, shape, scale, reach, cuts=(), kind=jnp.bfloat16):
    factor_of = level_of(key, shape, cuts, -0.22, 0.18) if cuts else 1.0
    entries = jax.random.normal(key, shape, jnp.float32) * scale * factor_of
    return jnp.minimum(jnp.maximum(entries, -reach), reach).astype(kind)


def setup_inputs(seed: int = 0) -> dict:
    splits = jax.random.split(jax.random.key(seed), 9)
    leaf_basis = scatter_about(splits[0], (NLEAF, LEAF, BASIS_RANK), LEAF ** -0.5, 0.5, ((0, 512),), jnp.float32)
    local_transfer = scatter_about(splits[1], (NLOCAL, BASIS_RANK, BASIS_RANK), (2 * BASIS_RANK) ** -0.5, 0.5, ((0, 512),))
    col_transfer = scatter_about(splits[2], (N_ROW, 2 * N_COL - 2, BASIS_RANK, BASIS_RANK), (2 * BASIS_RANK) ** -0.5, 0.5, ((0, 256),))
    row_transfer = draw_row_transfer(jax.random.fold_in(splits[8], 71), 0)
    coupling = scatter_about(splits[4], (TOTAL_SLOTS, BASIS_RANK, BASIS_RANK), 1.0, 6.0, ((0, 512),))
    slot_block_row = draw_slot_block_row(jax.random.fold_in(splits[8], 71), 0)
    block_col = draw_block_col(jax.random.fold_in(splits[8], 71), 0)
    block_valid = draw_block_valid(jax.random.fold_in(splits[8], 71), 0)
    return {"leaf_basis": leaf_basis, "local_transfer": local_transfer, "col_transfer": col_transfer, "row_transfer": row_transfer, "coupling": coupling, "slot_block_row": slot_block_row, "block_col": block_col, "block_valid": block_valid}


HIGH = lax.Precision.HIGHEST

def upper_chol(stacked):
    gram_matrix = jnp.einsum('...mk,...ml->...kl', stacked, stacked, precision=HIGH)
    cholesky_lower = jnp.linalg.cholesky(gram_matrix)
    return jnp.swapaxes(cholesky_lower, -1, -2)

def merge_pairs(factors, transfers):
    scaled = jnp.einsum('...nij,...njl->...nil', factors, transfers.astype(jnp.float32), precision=HIGH)
    extent = scaled.shape
    stacked = scaled.reshape(extent[:-3] + (extent[-3] // 2, 2 * extent[-2], extent[-1]))
    return upper_chol(stacked)

def project(rows_f, cols_f, blocks, valid_mask):
    left_product = jnp.einsum('bij,bjl->bil', rows_f, blocks.astype(jnp.float32), precision=HIGH)
    outcome = jnp.einsum('bil,bml->bim', left_product, cols_f, precision=HIGH)
    return jnp.where(valid_mask[:, None, None] == 1, outcome, 0.0).astype(jnp.bfloat16)

def reference(leaf_basis, local_transfer, col_transfer, row_transfer, coupling, slot_block_row, block_col, block_valid):
    devices_all = N_ROW * N_COL
    width = BASIS_RANK
    level_now = upper_chol(leaf_basis.reshape(devices_all, LEAF_DEV, LEAF, width))
    factors = [level_now]
    local_table = local_transfer.reshape(devices_all, 2 * LEAF_DEV - 2, width, width)
    offset = 0
    members = LEAF_DEV
    while members > 1:
        level_now = merge_pairs(level_now, local_table[:, offset:offset + members])
        offset += members
        members //= 2
        factors.append(level_now)
    present_level = level_now[:, 0].reshape(N_ROW, N_COL, width, width)
    parent_chain = []
    offset = 0
    members = N_COL
    while members > 1:
        present_level = merge_pairs(present_level, col_transfer[:, offset:offset + members])
        offset += members
        members //= 2
        parent_chain.append(jnp.repeat(present_level, N_COL // members, axis=1).reshape(devices_all, width, width))
    present_level = present_level[:, 0]
    for height in range(RLEV):
        present_level = merge_pairs(present_level, row_transfer[::2 ** height, height])
        spread = jnp.repeat(present_level, 2 ** (height + 1), axis=0)
        parent_chain.append(jnp.repeat(spread[:, None], N_COL, axis=1).reshape(devices_all, width, width))
    path_factor = jnp.stack(parent_chain, axis=1)
    per_cluster = coupling.shape[0] // (devices_all * (2 * LEAF_DEV - 1))
    slots_dev = per_cluster * (2 * LEAF_DEV - 1)
    blocks_all = coupling.reshape(devices_all, slots_dev, width, width)
    rows_all = slot_block_row.reshape(devices_all, slots_dev)
    cols_all = block_col.reshape(devices_all, slots_dev)
    valid_all = block_valid.reshape(devices_all, slots_dev)
    col_tables = [tier.reshape(N_ROW, N_COL * tier.shape[1], width, width) for tier in factors]

    def device_blocks(device):
        subtree = device // N_COL
        before = (subtree + N_ROW - 1) % N_ROW
        after = (subtree + 1) % N_ROW
        pieces = []
        leading_slot = 0
        for height in range(len(factors)):
            slots = per_cluster * (LEAF_DEV // 2 ** height)
            table = col_tables[height]
            neighbours = jnp.concatenate([table[before], table[subtree], table[after]], axis=0)
            rows_f = jnp.take(factors[height][device], rows_all[device, leading_slot:leading_slot + slots], axis=0)
            cols_f = jnp.take(neighbours, cols_all[device, leading_slot:leading_slot + slots], axis=0)
            pieces.append(project(rows_f, cols_f, blocks_all[device, leading_slot:leading_slot + slots], valid_all[device, leading_slot:leading_slot + slots]))
            leading_slot += slots
        return jnp.concatenate(pieces, axis=0)
    projected = lax.map(device_blocks, jnp.arange(devices_all, dtype=jnp.int32))
    return (projected.reshape(coupling.shape), path_factor)
```

```python
import functools

import jax
import jax.numpy as jnp
from jax import lax
from jax.experimental import pallas as pl
from jax.experimental.pallas import tpu as pltpu
from jax.sharding import PartitionSpec as P

BF = jnp.bfloat16
F32 = jnp.float32
NT = (((1,), (1,)), ((), ()))
MESH = pl.DeviceIdType.MESH
VMEM = pl.BlockSpec(memory_space=pltpu.VMEM)
SMEM = pl.BlockSpec(memory_space=pltpu.SMEM)

LEVELS = ((0, 128, 3, 0), (128, 64, 2, 8), (192, 32, 1, 12), (224, 16, 0, 14))
ROUNDS = ((0, 2), (2, 5), (5, 8))
ENTRIES = 16


def split2(x):
    high = x.astype(BF)
    return high, (x - high.astype(F32)).astype(BF)


def split3(x):
    high = x.astype(BF)
    rest = x - high.astype(F32)
    middle = rest.astype(BF)
    return high, middle, (rest - middle.astype(F32)).astype(BF)


def gram(xt):
    h, m, l = split3(xt)
    left = jnp.concatenate([h, h, m, h, l, m], axis=1)
    right = jnp.concatenate([h, m, h, l, h, m], axis=1)
    return lax.dot_general(left, right, NT, preferred_element_type=F32)


def tripled(transfer):
    et = transfer.astype(F32).T.astype(BF)
    return jnp.concatenate([et, et, et], axis=1)


def sandwich(et3, g):
    y = lax.dot_general(et3, jnp.concatenate(split3(g), axis=1), NT, preferred_element_type=F32)
    return lax.dot_general(jnp.concatenate(split3(y), axis=1), et3, NT, preferred_element_type=F32)


def folded(g):
    return jnp.concatenate([g[:32], g[32:]], axis=1)


def unfolded(g):
    return jnp.concatenate([g[:, :64], g[:, 64:]], axis=0)


def pick(row, lane):
    lanes = lax.broadcasted_iota(jnp.int32, row.shape, 1)
    index = jnp.where(lanes < 64, lane, 64 + lane)
    return jnp.take_along_axis(row, index, axis=1, mode="promise_in_bounds")


def chol_pack(a_ref, u_ref, size=64, width=8):
    column = lax.broadcasted_iota(jnp.int32, (8, 128), 1) % 64
    for first in range(0, size, width):
        rows = [a_ref[first + i] for i in range(width)]
        for m in range(first):
            done = u_ref[m]
            for i in range(width):
                rows[i] = rows[i] - pick(done, first + i) * done
        entry = {}
        for i in range(width):
            for j in range(i, width):
                entry[i, j] = pick(rows[i], first + j)
        for k in range(width):
            scale = lax.rsqrt(entry[k, k])
            top = rows[k] * scale
            u_ref[first + k] = jnp.where(column < first + k, 0.0, top)
            factor = {j: entry[k, j] * scale for j in range(k + 1, width)}
            for i in range(k + 1, width):
                rows[i] = rows[i] - factor[i] * top
                for j in range(i, width):
                    entry[i, j] = entry[i, j] - factor[i] * factor[j]


def local_kernel(leaf_ref, transfer_ref, u_ref, root_ref, a_ref, et_ref):
    for i in range(14):
        et_ref[i] = tripled(transfer_ref[i])
    level = [gram(leaf_ref[i]) for i in range(8)]
    grams = list(level)
    offset = 0
    while len(level) > 1:
        parts = [sandwich(et_ref[offset + i], g) for i, g in enumerate(level)]
        offset += len(level)
        level = [parts[i] + parts[i + 1] for i in range(0, len(parts), 2)]
        grams += level
    root_ref[...] = level[0]
    row = lax.broadcasted_iota(jnp.int32, (64, 64), 0)
    column = lax.broadcasted_iota(jnp.int32, (64, 64), 1)
    grams.append(jnp.where(row == column, 1.0, 0.0))
    for b in range(8):
        a_ref[:, b, :] = jnp.concatenate([grams[b], grams[8 + b]], axis=1)
    chol_pack(a_ref, u_ref)


def partners(row, rounds):
    found = []
    for low, high in rounds:
        for d in range(1, 1 << (high - low)):
            block = 1 << low
            digit = row // block % (1 << (high - low))
            flipped = 0
            for bit in range(high - low):
                own = digit // (1 << bit) % 2
                flipped = flipped + ((1 - own) if d >> bit & 1 else own) * (1 << bit)
            found.append(row + (flipped - digit) * block)
    return found


def exchange_kernel(u_ref, root_ref, col_ref, path_ref, tables_ref, grams_ref,
                    et_ref, out_buf, in_buf, send_sem, recv_sem, tab_send, tab_recv):
    row = lax.axis_index("row")
    col = lax.axis_index("col")
    rows = lax.axis_size("row")
    after = lax.rem(row + 1, rows)
    before = lax.rem(row + rows - 1, rows)
    others = partners(row, ROUNDS)
    mate = (row, 1 - col)

    barrier = pltpu.get_barrier_semaphore()
    for device in [mate, (before, col), (after, col)] + [(r, col) for r in others]:
        pl.semaphore_signal(barrier, inc=1, device_id=device, device_id_type=MESH)

    et_ref[8] = tripled(col_ref[col])
    for k in range(8):
        et_ref[k] = tripled(path_ref[k])
    part = folded(sandwich(et_ref[8], root_ref[...]))
    out_buf[0] = part
    pl.semaphore_wait(barrier, 3 + len(others))

    def send(slot, target, place):
        copy = pltpu.make_async_remote_copy(
            src_ref=out_buf.at[slot], dst_ref=in_buf.at[place],
            send_sem=send_sem.at[place], recv_sem=recv_sem.at[place],
            device_id=target, device_id_type=MESH)
        copy.start()
        return copy

    def table(source, place, sem, target):
        copy = pltpu.make_async_remote_copy(
            src_ref=source, dst_ref=tables_ref.at[place],
            send_sem=tab_send.at[sem], recv_sem=tab_recv.at[sem],
            device_id=target, device_id_type=MESH)
        copy.start()
        return copy

    chain = [send(0, mate, 0)]
    to_after = table(u_ref, 0 + col, 0, (after, col))
    to_before = table(u_ref, 4 + col, 1, (before, col))
    to_mate = table(u_ref, 2 + col, 2, mate)
    tables_ref[2 + col] = u_ref[...]

    chain[0].wait_recv()
    total = part + in_buf[0]
    grams = [unfolded(total)]
    place = 1
    slot = 1
    for low, high in ROUNDS:
        own = grams[-1]
        parts = []
        first = place
        for t in range(1, high - low + 1):
            own = sandwich(et_ref[low + t - 1], own)
            parts.append(folded(own))
            out_buf[slot] = parts[-1]
            for d in range(1 << (t - 1), 1 << t):
                chain.append(send(slot, (others[place - 1], col), place))
                place += 1
            slot += 1
        place = first
        for t in range(1, high - low + 1):
            if t == 1:
                total = parts[0]
            else:
                total = folded(sandwich(et_ref[low + t - 1], grams[-1]))
            for d in range(1 << (t - 1), 1 << t):
                chain[place].wait_recv()
                total = total + in_buf[place]
                place += 1
            grams.append(unfolded(total))
    unit = jnp.where(lax.broadcasted_iota(jnp.int32, (64, 64), 0)
                     == lax.broadcasted_iota(jnp.int32, (64, 64), 1), 1.0, 0.0)
    for b in range(8):
        grams_ref[:, b, :] = jnp.concatenate([grams[b], grams[8] if b == 0 else unit], axis=1)

    to_after.wait_recv()
    from_before = table(tables_ref.at[0 + col], 0 + col, 3, mate)
    to_before.wait_recv()
    from_after = table(tables_ref.at[4 + col], 4 + col, 4, mate)
    for copy in (to_mate, from_before, from_after):
        copy.wait_recv()
    for copy in (to_after, to_before, to_mate, from_before, from_after):
        copy.wait_send()
    for copy in chain:
        copy.wait_send()


def project_kernel(rows_ref, cols_ref, ct_ref, valid_ref, tables_ref, own_ref, grams_ref, out_ref, path_ref,
                   t_ref, o_ref, left_ref, right_ref, u_ref):
    chol_pack(grams_ref, u_ref)
    for k in range(9):
        path_ref[0, k] = u_ref[:, k % 8, (k // 8) * 64:(k // 8) * 64 + 64]

    def unpack(t, carry):
        for b in range(8):
            both = tables_ref[t, :, b, :]
            for half in range(2):
                h, l = split2(both[:, half * 64:half * 64 + 64])
                right_ref[t * ENTRIES + half * 8 + b] = jnp.concatenate([h, l], axis=1)
        return carry

    lax.fori_loop(0, 6, unpack, 0)
    for b in range(8):
        both = own_ref[:, b, :]
        for half in range(2):
            h, l = split2(both[:, half * 64:half * 64 + 64])
            left_ref[half * 8 + b] = jnp.concatenate([h, l, h], axis=1)

    def spread(p, carry):
        x = jnp.concatenate([ct_ref[p].astype(F32), ct_ref[p + 32].astype(F32)], axis=0)
        t_ref[p] = x.T
        return carry

    lax.fori_loop(0, 32, spread, 0, unroll=2)

    for first, slots, log_n, offset in LEVELS:
        unroll = min(slots, 64)

        def group(g, carry):
            for k in range(unroll):
                s = first + g * unroll + k
                r = rows_ref[s] + offset
                v = cols_ref[s]
                q = (v >> log_n) * ENTRIES + offset + (v & ((1 << log_n) - 1))
                c = t_ref[:, s, :].astype(BF)
                top = jnp.concatenate([c[:, :64], c[:, :64]], axis=1)
                low = jnp.concatenate([c[:, 64:], c[:, 64:]], axis=1)
                y = lax.dot_general(right_ref[q], jnp.concatenate([top, low], axis=0), NT,
                                    preferred_element_type=F32)
                h, l = split2(y)
                o = lax.dot_general(left_ref[r], jnp.concatenate([h, h, l], axis=1), NT,
                                    preferred_element_type=F32)
                o_ref[:, s, :] = folded(o)
            return carry

        lax.fori_loop(0, slots // unroll, group, 0)

    real = valid_ref[...] == 1

    def gather(p, carry):
        x = jnp.where(real, o_ref[p].T, 0.0).astype(BF)
        out_ref[p] = x[:64]
        out_ref[p + 32] = x[64:]
        return carry

    lax.fori_loop(0, 32, gather, 0, unroll=2)


def shards(leaf_basis, local_transfer, col_transfer, row_transfer, coupling, slot_block_row, block_col, block_valid):
    pack = jax.ShapeDtypeStruct((64, 8, 128), F32)
    limit = pltpu.CompilerParams(vmem_limit_bytes=56 * 2**20)
    factors, root = pl.pallas_call(
        local_kernel,
        out_shape=(pack, jax.ShapeDtypeStruct((64, 64), F32)),
        in_specs=[VMEM] * 2,
        out_specs=(VMEM, VMEM),
        scratch_shapes=[pltpu.VMEM((64, 8, 128), F32), pltpu.VMEM((14, 64, 192), BF)],
        compiler_params=limit,
        name="local_factors",
    )(leaf_basis.transpose(0, 2, 1), local_transfer)
    slots = 1 + sum((1 << (high - low)) - 1 for low, high in ROUNDS)
    tables, grams = pl.pallas_call(
        exchange_kernel,
        out_shape=(jax.ShapeDtypeStruct((6, 64, 8, 128), F32), pack),
        in_specs=[VMEM] * 4,
        out_specs=(VMEM, VMEM),
        scratch_shapes=[
            pltpu.VMEM((9, 64, 192), BF),
            pltpu.VMEM((9, 32, 128), F32),
            pltpu.VMEM((slots, 32, 128), F32),
            pltpu.SemaphoreType.DMA((slots,)),
            pltpu.SemaphoreType.DMA((slots,)),
            pltpu.SemaphoreType.DMA((5,)),
            pltpu.SemaphoreType.DMA((5,)),
        ],
        compiler_params=pltpu.CompilerParams(
            vmem_limit_bytes=56 * 2**20, collective_id=0, has_side_effects=True),
        name="exchange",
    )(factors, root, col_transfer[0], row_transfer[0])
    projected, path_factor = pl.pallas_call(
        project_kernel,
        out_shape=(jax.ShapeDtypeStruct((64, 64, 240), BF), jax.ShapeDtypeStruct((1, 9, 64, 64), F32)),
        in_specs=[SMEM, SMEM] + [VMEM] * 5,
        out_specs=(VMEM, VMEM),
        scratch_shapes=[
            pltpu.VMEM((32, 240, 128), F32),
            pltpu.VMEM((32, 240, 128), F32),
            pltpu.VMEM((ENTRIES, 64, 192), BF),
            pltpu.VMEM((6 * ENTRIES, 64, 128), BF),
            pltpu.VMEM((64, 8, 128), F32),
        ],
        compiler_params=limit,
        name="project",
    )(slot_block_row, block_col, coupling.transpose(1, 2, 0), block_valid[None], tables, factors, grams)
    return projected.transpose(2, 0, 1), path_factor


def solution(mesh):
    placed = (
        P(("row", "col"), None, None),
        P(("row", "col"), None, None),
        P("row", None, None, None),
        P("row", None, None, None),
        P(("row", "col"), None, None),
        P(("row", "col")),
        P(("row", "col")),
        P(("row", "col")),
    )
    return jax.shard_map(
        shards,
        mesh=mesh,
        in_specs=placed,
        out_specs=(P(("row", "col"), None, None), P(("row", "col"), None, None, None)),
        check_vma=False,
    )
```

```python
import functools

import jax
import jax.numpy as jnp
from jax import lax
from jax.experimental import pallas as pl
from jax.experimental.pallas import tpu as pltpu
from jax.sharding import PartitionSpec as P

BF = jnp.bfloat16
F32 = jnp.float32
NT = (((1,), (1,)), ((), ()))
MESH = pl.DeviceIdType.MESH
VMEM = pl.BlockSpec(memory_space=pltpu.VMEM)
SMEM = pl.BlockSpec(memory_space=pltpu.SMEM)

PAIRS = ((0, 64, 2, 8), (64, 32, 1, 12), (96, 16, 0, 14), (112, 16, None, 0))
ROUNDS = ((0, 2), (2, 5), (5, 8))
COL = 14
PATH = 15
GROUP = 16
PACKED = 33


def split2(x):
    high = x.astype(BF)
    return high, (x - high.astype(F32)).astype(BF)


def split3(x):
    high = x.astype(BF)
    rest = x - high.astype(F32)
    middle = rest.astype(BF)
    return high, middle, (rest - middle.astype(F32)).astype(BF)


def dot_nt(a, b):
    return lax.dot_general(a, b, NT, preferred_element_type=F32)


def gram(xt):
    h, m, l = split3(xt)
    left = jnp.concatenate([h, h, m, h, l, m], axis=1)
    right = jnp.concatenate([h, m, h, l, h, m], axis=1)
    return lax.dot_general(left, right, NT, preferred_element_type=F32)


def tripled(transfer):
    et = transfer.astype(F32).T.astype(BF)
    return jnp.concatenate([et, et, et], axis=1)


def sandwich(et3, g):
    y = lax.dot_general(et3, jnp.concatenate(split3(g), axis=1), NT, preferred_element_type=F32)
    return lax.dot_general(jnp.concatenate(split3(y), axis=1), et3, NT, preferred_element_type=F32)


def folded(g):
    return jnp.concatenate([g[:32], g[32:]], axis=1)


def unfolded(g):
    return jnp.concatenate([g[:, :64], g[:, 64:]], axis=0)


def take(row, index):
    return jnp.take_along_axis(row, index, axis=1, mode="promise_in_bounds")


def factor_blocks(a_ref, u_ref, low, high):
    lane = lax.broadcasted_iota(jnp.int32, (8, 128), 1)
    half = lane // 64 * 64
    column = lane % 64

    def block(number, carry):
        first = number * 8
        index = [half + (first + i) for i in range(8)]

        def update(g, rows):
            done = [u_ref[g * 8 + m] for m in range(8)]
            fresh = []
            for i in range(8):
                terms = [take(done[m], index[i]) * done[m] for m in range(8)]
                while len(terms) > 1:
                    terms = [terms[k] + terms[k + 1] for k in range(0, len(terms), 2)]
                fresh.append(rows[i] - terms[0])
            return tuple(fresh)

        rows = list(lax.fori_loop(0, number, update, tuple(a_ref[first + i] for i in range(8))))
        entry = {}
        for j in range(8):
            for i in range(j + 1):
                entry[i, j] = take(rows[i], index[j])
        for k in range(8):
            scale = lax.rsqrt(entry[k, k])
            top = rows[k] * scale
            u_ref[first + k] = jnp.where(column < first + k, 0.0, top)
            factor = {j: entry[k, j] * scale for j in range(k + 1, 8)}
            for i in range(k + 1, 8):
                rows[i] = rows[i] - factor[i] * top
                for j in range(i, 8):
                    entry[i, j] = entry[i, j] - factor[i] * factor[j]
        return carry

    lax.fori_loop(low, high, block, 0)


def partners(row, rounds):
    found = []
    for low, high in rounds:
        for d in range(1, 1 << (high - low)):
            block = 1 << low
            digit = row // block % (1 << (high - low))
            flipped = 0
            for bit in range(high - low):
                own = digit // (1 << bit) % 2
                flipped = flipped + ((1 - own) if d >> bit & 1 else own) * (1 << bit)
            found.append(row + (flipped - digit) * block)
    return found


def local_grams(leaf_ref, et_ref):
    level = [gram(leaf_ref[i]) for i in range(8)]
    grams = list(level)
    offset = 0
    while len(level) > 1:
        parts = [sandwich(et_ref[offset + i], g) for i, g in enumerate(level)]
        offset += len(level)
        level = [parts[i] + parts[i + 1] for i in range(0, len(parts), 2)]
        grams += level
    return grams


def pack_triangles(u_ref, packed_ref):
    column = lax.broadcasted_iota(jnp.int32, (8, 128), 1) % 64
    packed_ref[0] = u_ref[0]
    packed_ref[32] = u_ref[32]
    for i in range(1, 32):
        packed_ref[i] = jnp.where(column >= i, u_ref[i], pltpu.roll(u_ref[64 - i], i, 1))


def unpack_triangles(packed_ref, u_ref):
    column = lax.broadcasted_iota(jnp.int32, (8, 128), 1) % 64
    u_ref[0] = packed_ref[0]
    u_ref[32] = packed_ref[32]
    for i in range(1, 32):
        both = packed_ref[i]
        u_ref[i] = jnp.where(column >= i, both, 0.0)
        u_ref[64 - i] = pltpu.roll(jnp.where(column >= i, 0.0, both), 128 - i, 1)


def main_kernel(rows_ref, cols_ref, leaf_ref, local_ref, col_ref, path_ref, ct_hbm, valid_ref, out_hbm, grams_ref,
                et_ref, a_ref, u_ref, g_ref, ct_ref, t_ref, o_ref, out_ref, table_ref, full_ref, left_ref, low_ref,
                high_ref, out_buf, in_buf, send_sem, recv_sem, tab_send, tab_recv, local_sem):
    row = lax.axis_index("row")
    col = lax.axis_index("col")
    rows = lax.axis_size("row")
    after = lax.rem(row + 1, rows)
    before = lax.rem(row + rows - 1, rows)
    others = partners(row, ROUNDS)
    mate = (row, 1 - col)
    left = lax.broadcasted_iota(jnp.int32, (64, 128), 1) < 64

    fetch = pltpu.make_async_copy(ct_hbm, ct_ref, local_sem.at[0])
    fetch.start()
    barrier = pltpu.get_barrier_semaphore()
    for device in [mate, (before, col), (after, col)] + [(r, col) for r in others]:
        pl.semaphore_signal(barrier, inc=1, device_id=device, device_id_type=MESH)

    def send(slot, target, place):
        copy = pltpu.make_async_remote_copy(
            src_ref=out_buf.at[slot], dst_ref=in_buf.at[place],
            send_sem=send_sem.at[place], recv_sem=recv_sem.at[place],
            device_id=target, device_id_type=MESH)
        copy.start()
        return copy

    def send_table(place, sem, target, there):
        copy = pltpu.make_async_remote_copy(
            src_ref=table_ref.at[place], dst_ref=table_ref.at[there],
            send_sem=tab_send.at[sem], recv_sem=tab_recv.at[sem],
            device_id=target, device_id_type=MESH)
        copy.start()
        return copy

    chain = []
    starts = []
    for low, high in ROUNDS:
        starts.append((1 + sum((1 << (b - a)) - 1 for a, b in ROUNDS if a < low), low, high))

    def send_round(number):
        first, low, high = starts[number]
        own = g_ref[low]
        place = first
        for t in range(1, high - low + 1):
            own = sandwich(et_ref[PATH + low + t - 1], own)
            out_buf[low + t] = folded(own)
            for d in range(1 << (t - 1), 1 << t):
                chain.append(send(low + t, (others[place - 1], col), place))
                place += 1

    def end_round(number):
        first, low, high = starts[number]
        place = first
        for t in range(1, high - low + 1):
            if t == 1:
                total = out_buf[low + 1]
            else:
                total = folded(sandwich(et_ref[PATH + low + t - 1], g_ref[low + t - 1]))
            for d in range(1 << (t - 1), 1 << t):
                chain[place].wait_recv()
                total = total + in_buf[place]
                place += 1
            g_ref[low + t] = unfolded(total)

    for i in range(14):
        et_ref[i] = tripled(local_ref[i])
    et_ref[COL] = tripled(col_ref[col])
    grams = local_grams(leaf_ref, et_ref)
    out_buf[0] = folded(sandwich(et_ref[COL], grams[14]))
    pl.semaphore_wait(barrier, 3 + len(others))
    chain.append(send(0, mate, 0))

    unit = jnp.where(lax.broadcasted_iota(jnp.int32, (64, 64), 0)
                     == lax.broadcasted_iota(jnp.int32, (64, 64), 1), 1.0, 0.0)
    grams.append(unit)
    for b in range(8):
        a_ref[:, b, :] = jnp.concatenate([grams[b], grams[8 + b]], axis=1)
    for k in range(8):
        et_ref[PATH + k] = tripled(path_ref[k])
    chain[0].wait_recv()
    g_ref[0] = unfolded(out_buf[0] + in_buf[0])
    send_round(0)
    factor_blocks(a_ref, u_ref, 0, 5)
    end_round(0)
    send_round(1)
    factor_blocks(a_ref, u_ref, 5, 8)
    mine = 2 + col
    pack_triangles(u_ref, table_ref.at[mine])
    to_after = send_table(mine, 0, (after, col), col)
    to_before = send_table(mine, 1, (before, col), 4 + col)
    to_mate = send_table(mine, 2, mate, mine)
    end_round(1)
    send_round(2)

    fetch.wait()
    pad = jnp.zeros((64, 16), F32)

    def spread(j, carry):
        x = ct_ref[j].astype(F32)
        later = jnp.concatenate([x[:, 128:], pad], axis=1)
        t_ref[j] = jnp.concatenate([x[:, :128], later], axis=0).T
        return carry

    lax.fori_loop(0, 64, spread, 0, unroll=4)

    for b in range(8):
        both = u_ref[:, b, :]
        for half in range(2):
            x = jnp.concatenate(split2(both[:, half * 64:half * 64 + 64]), axis=1)
            left_ref[half * 8 + b] = jnp.concatenate([x, x], axis=1)

    to_after.wait_recv()
    from_before = send_table(col, 3, mate, col)
    to_before.wait_recv()
    from_after = send_table(4 + col, 4, mate, 4 + col)
    to_mate.wait_recv()
    from_before.wait_recv()
    from_after.wait_recv()

    def unpack(t, carry):
        unpack_triangles(table_ref.at[t], full_ref)
        for b in range(8):
            h, l = split2(full_ref[:, b, :])
            zero = jnp.zeros_like(h)
            low_ref[t * 8 + b] = jnp.concatenate([jnp.where(left, h, zero), jnp.where(left, l, zero)], axis=1)
            high_ref[t * 8 + b] = jnp.concatenate([jnp.where(left, zero, h), jnp.where(left, zero, l)], axis=1)
        return carry

    lax.fori_loop(0, 6, unpack, 0)

    for start, count, log_n, offset in PAIRS:
        def group(g, carry):
            for k in range(GROUP):
                p = start + g * GROUP + k
                v = cols_ref[p]
                right_a = low_ref[v]
                left_a = left_ref[rows_ref[p]]
                if log_n is None:
                    right_b = high_ref[0]
                    left_b = left_ref[0]
                else:
                    v = cols_ref[p + 128]
                    right_b = high_ref[(v >> log_n) * 8 + (offset - 8) + (v & ((1 << log_n) - 1))]
                    left_b = left_ref[rows_ref[p + 128] + offset]
                c = t_ref[:, p, :].astype(BF)
                c = jnp.concatenate([c, c], axis=1)
                y = dot_nt(jnp.concatenate([right_a, right_b], axis=0), jnp.concatenate([c, c], axis=0))
                o = dot_nt(jnp.concatenate([left_a, left_b], axis=0), jnp.concatenate(split2(y), axis=1))
                o_ref[:, p, :] = jnp.where(left, o[:64], o[64:])
            return carry

        lax.fori_loop(0, count // GROUP, group, 0)

    real = valid_ref[...] == 1

    def gather(i, carry):
        x = o_ref[i].T
        x = jnp.concatenate([x[:64], x[64:, :112]], axis=1)
        out_ref[i] = jnp.where(real, x, 0.0).astype(BF)
        return carry

    lax.fori_loop(0, 64, gather, 0, unroll=4)
    store = pltpu.make_async_copy(out_ref, out_hbm, local_sem.at[1])
    store.start()

    end_round(2)
    for b in range(8):
        grams_ref[:, b, :] = jnp.concatenate([g_ref[b], g_ref[8] if b == 0 else unit], axis=1)
    store.wait()
    for copy in (to_after, to_before, to_mate, from_before, from_after):
        copy.wait_send()
    for copy in chain:
        copy.wait_send()


def path_kernel(blocks_hbm, grams_ref, out_hbm, path_ref, u_ref, sem):
    copy = pltpu.make_async_copy(blocks_hbm, out_hbm, sem)
    copy.start()
    factor_blocks(grams_ref, u_ref, 0, 8)
    for k in range(9):
        path_ref[0, k] = u_ref[:, k % 8, (k // 8) * 64:(k // 8) * 64 + 64]
    copy.wait()


def shards(leaf_basis, local_transfer, col_transfer, row_transfer, coupling, slot_block_row, block_col, block_valid):
    blocks = jax.ShapeDtypeStruct((64, 64, 240), BF)
    places = 1 + sum((1 << (high - low)) - 1 for low, high in ROUNDS)
    hbm = pl.BlockSpec(memory_space=pl.ANY)
    projected, grams = pl.pallas_call(
        main_kernel,
        out_shape=(blocks, jax.ShapeDtypeStruct((64, 8, 128), F32)),
        in_specs=[SMEM, SMEM, VMEM, VMEM, VMEM, VMEM, hbm, VMEM],
        out_specs=(hbm, VMEM),
        scratch_shapes=[
            pltpu.VMEM((23, 64, 192), BF),
            pltpu.VMEM((64, 8, 128), F32),
            pltpu.VMEM((64, 8, 128), F32),
            pltpu.VMEM((9, 64, 64), F32),
            pltpu.VMEM((64, 64, 240), BF),
            pltpu.VMEM((64, 128, 128), F32),
            pltpu.VMEM((64, 128, 128), F32),
            pltpu.VMEM((64, 64, 240), BF),
            pltpu.VMEM((6, PACKED, 8, 128), F32),
            pltpu.VMEM((64, 8, 128), F32),
            pltpu.VMEM((16, 64, 256), BF),
            pltpu.VMEM((48, 64, 256), BF),
            pltpu.VMEM((48, 64, 256), BF),
            pltpu.VMEM((9, 32, 128), F32),
            pltpu.VMEM((places, 32, 128), F32),
            pltpu.SemaphoreType.DMA((places,)),
            pltpu.SemaphoreType.DMA((places,)),
            pltpu.SemaphoreType.DMA((5,)),
            pltpu.SemaphoreType.DMA((5,)),
            pltpu.SemaphoreType.DMA((2,)),
        ],
        compiler_params=pltpu.CompilerParams(
            vmem_limit_bytes=60 * 2**20, collective_id=0, has_side_effects=True),
        name="upsweep_and_projection",
    )(slot_block_row, block_col, leaf_basis.transpose(0, 2, 1), local_transfer, col_transfer[0], row_transfer[0],
      coupling.transpose(1, 2, 0), block_valid[None])
    projected, path_factor = pl.pallas_call(
        path_kernel,
        out_shape=(blocks, jax.ShapeDtypeStruct((1, 9, 64, 64), F32)),
        in_specs=[hbm, VMEM],
        out_specs=(hbm, VMEM),
        scratch_shapes=[pltpu.VMEM((64, 8, 128), F32), pltpu.SemaphoreType.DMA(())],
        compiler_params=pltpu.CompilerParams(vmem_limit_bytes=60 * 2**20),
        name="path_factors",
    )(projected, grams)
    return projected.transpose(2, 0, 1), path_factor


def solution(mesh):
    placed = (
        P(("row", "col"), None, None),
        P(("row", "col"), None, None),
        P("row", None, None, None),
        P("row", None, None, None),
        P(("row", "col"), None, None),
        P(("row", "col")),
        P(("row", "col")),
        P(("row", "col")),
    )
    return jax.shard_map(
        shards,
        mesh=mesh,
        in_specs=placed,
        out_specs=(P(("row", "col"), None, None), P(("row", "col"), None, None, None)),
        check_vma=False,
    )
```

```python
import functools

import jax
import jax.numpy as jnp
from jax import lax
from jax.experimental import pallas as pl
from jax.experimental.pallas import tpu as pltpu
from jax.sharding import PartitionSpec as P

BF = jnp.bfloat16
F32 = jnp.float32
NT = (((1,), (1,)), ((), ()))
MESH = pl.DeviceIdType.MESH
VMEM = pl.BlockSpec(memory_space=pltpu.VMEM)
SMEM = pl.BlockSpec(memory_space=pltpu.SMEM)

PAIRS = ((0, 64, 2, 8), (64, 32, 1, 12), (96, 16, 0, 14), (112, 16, None, None))
ROUNDS = ((0, 2), (2, 5), (5, 8))
COL = 14
PATH = 15
GROUP = 32
PACKED = 33


def split2(x):
    high = x.astype(BF)
    return high, (x - high.astype(F32)).astype(BF)


def split3(x):
    high = x.astype(BF)
    rest = x - high.astype(F32)
    middle = rest.astype(BF)
    return high, middle, (rest - middle.astype(F32)).astype(BF)


def dot_nt(a, b):
    return lax.dot_general(a, b, NT, preferred_element_type=F32)


def gram(xt):
    h, m, l = split3(xt)
    left = jnp.concatenate([h, h, m, h, l, m], axis=1)
    right = jnp.concatenate([h, m, h, l, h, m], axis=1)
    return lax.dot_general(left, right, NT, preferred_element_type=F32)


def tripled(transfer):
    et = transfer.astype(F32).T.astype(BF)
    return jnp.concatenate([et, et, et], axis=1)


def sandwich(et3, g):
    y = lax.dot_general(et3, jnp.concatenate(split3(g), axis=1), NT, preferred_element_type=F32)
    return lax.dot_general(jnp.concatenate(split3(y), axis=1), et3, NT, preferred_element_type=F32)


def folded(g):
    return jnp.concatenate([g[:32], g[32:]], axis=1)


def unfolded(g):
    return jnp.concatenate([g[:, :64], g[:, 64:]], axis=0)


def take(row, index):
    return jnp.take_along_axis(row, index, axis=1, mode="promise_in_bounds")


def factor_blocks(a_ref, u_ref, low, high):
    lane = lax.broadcasted_iota(jnp.int32, (8, 128), 1)
    half = lane // 64 * 64
    column = lane % 64

    def block(number, carry):
        first = number * 8
        index = [half + (first + i) for i in range(8)]

        def update(g, rows):
            done = [u_ref[g * 8 + m] for m in range(8)]
            fresh = []
            for i in range(8):
                terms = [take(done[m], index[i]) * done[m] for m in range(8)]
                while len(terms) > 1:
                    terms = [terms[k] + terms[k + 1] for k in range(0, len(terms), 2)]
                fresh.append(rows[i] - terms[0])
            return tuple(fresh)

        rows = list(lax.fori_loop(0, number, update, tuple(a_ref[first + i] for i in range(8))))
        entry = {}
        for j in range(8):
            for i in range(j + 1):
                entry[i, j] = take(rows[i], index[j])
        for k in range(8):
            scale = lax.rsqrt(entry[k, k])
            top = rows[k] * scale
            u_ref[first + k] = jnp.where(column < first + k, 0.0, top)
            factor = {j: entry[k, j] * scale for j in range(k + 1, 8)}
            for i in range(k + 1, 8):
                rows[i] = rows[i] - factor[i] * top
                for j in range(i, 8):
                    entry[i, j] = entry[i, j] - factor[i] * factor[j]
        return carry

    lax.fori_loop(low, high, block, 0)


def partners(row, rounds):
    found = []
    for low, high in rounds:
        for d in range(1, 1 << (high - low)):
            block = 1 << low
            digit = row // block % (1 << (high - low))
            flipped = 0
            for bit in range(high - low):
                own = digit // (1 << bit) % 2
                flipped = flipped + ((1 - own) if d >> bit & 1 else own) * (1 << bit)
            found.append(row + (flipped - digit) * block)
    return found


def local_grams(leaf_ref, et_ref):
    level = [gram(leaf_ref[i]) for i in range(8)]
    grams = list(level)
    offset = 0
    while len(level) > 1:
        parts = [sandwich(et_ref[offset + i], g) for i, g in enumerate(level)]
        offset += len(level)
        level = [parts[i] + parts[i + 1] for i in range(0, len(parts), 2)]
        grams += level
    return grams


def pack_triangles(u_ref, packed_ref):
    column = lax.broadcasted_iota(jnp.int32, (8, 128), 1) % 64
    packed_ref[0] = u_ref[0]
    packed_ref[32] = u_ref[32]
    for i in range(1, 32):
        packed_ref[i] = jnp.where(column >= i, u_ref[i], pltpu.roll(u_ref[64 - i], i, 1))


def unpack_triangles(packed_ref, u_ref):
    column = lax.broadcasted_iota(jnp.int32, (8, 128), 1) % 64
    u_ref[0] = packed_ref[0]
    u_ref[32] = packed_ref[32]
    for i in range(1, 32):
        both = packed_ref[i]
        u_ref[i] = jnp.where(column >= i, both, 0.0)
        u_ref[64 - i] = pltpu.roll(jnp.where(column >= i, 0.0, both), 128 - i, 1)


def main_kernel(rows_ref, cols_ref, leaf_ref, local_ref, col_ref, path_ref, ct_hbm, valid_ref, out_hbm, grams_ref,
                et_ref, a_ref, u_ref, g_ref, ct_ref, t_ref, o_ref, y_ref, out_ref, table_ref, full_ref, left_ref, low_ref,
                high_ref, out_buf, in_buf, send_sem, recv_sem, tab_send, tab_recv, local_sem):
    row = lax.axis_index("row")
    col = lax.axis_index("col")
    rows = lax.axis_size("row")
    after = lax.rem(row + 1, rows)
    before = lax.rem(row + rows - 1, rows)
    others = partners(row, ROUNDS)
    mate = (row, 1 - col)
    left = lax.broadcasted_iota(jnp.int32, (64, 128), 1) < 64

    fetch = pltpu.make_async_copy(ct_hbm, ct_ref, local_sem.at[0])
    fetch.start()
    barrier = pltpu.get_barrier_semaphore()
    for device in [mate, (before, col), (after, col)] + [(r, col) for r in others]:
        pl.semaphore_signal(barrier, inc=1, device_id=device, device_id_type=MESH)

    def send(slot, target, place):
        copy = pltpu.make_async_remote_copy(
            src_ref=out_buf.at[slot], dst_ref=in_buf.at[place],
            send_sem=send_sem.at[place], recv_sem=recv_sem.at[place],
            device_id=target, device_id_type=MESH)
        copy.start()
        return copy

    def send_table(place, sem, target, there):
        copy = pltpu.make_async_remote_copy(
            src_ref=table_ref.at[place], dst_ref=table_ref.at[there],
            send_sem=tab_send.at[sem], recv_sem=tab_recv.at[sem],
            device_id=target, device_id_type=MESH)
        copy.start()
        return copy

    chain = []
    starts = []
    for low, high in ROUNDS:
        starts.append((1 + sum((1 << (b - a)) - 1 for a, b in ROUNDS if a < low), low, high))

    def send_round(number):
        first, low, high = starts[number]
        own = g_ref[low]
        place = first
        for t in range(1, high - low + 1):
            own = sandwich(et_ref[PATH + low + t - 1], own)
            out_buf[low + t] = folded(own)
            for d in range(1 << (t - 1), 1 << t):
                chain.append(send(low + t, (others[place - 1], col), place))
                place += 1

    def end_round(number):
        first, low, high = starts[number]
        place = first
        for t in range(1, high - low + 1):
            if t == 1:
                total = out_buf[low + 1]
            else:
                total = folded(sandwich(et_ref[PATH + low + t - 1], g_ref[low + t - 1]))
            for d in range(1 << (t - 1), 1 << t):
                chain[place].wait_recv()
                total = total + in_buf[place]
                place += 1
            g_ref[low + t] = unfolded(total)

    def store_table(t):
        for b in range(8):
            x = full_ref[:, b, :]
            low_ref[t * 8 + b] = jnp.concatenate(split2(jnp.where(left, x, 0.0)), axis=1)
            high_ref[t * 8 + b] = jnp.concatenate(split2(jnp.where(left, 0.0, x)), axis=1)

    for i in range(14):
        et_ref[i] = tripled(local_ref[i])
    et_ref[COL] = tripled(col_ref[col])
    grams = local_grams(leaf_ref, et_ref)
    out_buf[0] = folded(sandwich(et_ref[COL], grams[14]))
    pl.semaphore_wait(barrier, 3 + len(others))
    chain.append(send(0, mate, 0))

    unit = jnp.where(lax.broadcasted_iota(jnp.int32, (64, 64), 0)
                     == lax.broadcasted_iota(jnp.int32, (64, 64), 1), 1.0, 0.0)
    grams.append(unit)
    for b in range(8):
        a_ref[:, b, :] = jnp.concatenate([grams[b], grams[8 + b]], axis=1)
    for k in range(8):
        et_ref[PATH + k] = tripled(path_ref[k])

    fetch.wait()
    pad = jnp.zeros((64, 16), F32)

    def spread(j, carry):
        x = ct_ref[j].astype(F32)
        later = jnp.concatenate([x[:, 128:], pad], axis=1)
        t_ref[:, j, :] = jnp.concatenate([x[:, :128], later], axis=0).T
        return carry

    lax.fori_loop(0, 64, spread, 0, unroll=4)

    chain[0].wait_recv()
    g_ref[0] = unfolded(out_buf[0] + in_buf[0])
    send_round(0)

    factor_blocks(a_ref, u_ref, 0, 8)
    mine = 2 + col
    pack_triangles(u_ref, table_ref.at[mine])
    to_after = send_table(mine, 0, (after, col), col)
    to_before = send_table(mine, 1, (before, col), 4 + col)
    to_mate = send_table(mine, 2, mate, mine)
    end_round(0)
    send_round(1)

    for b in range(8):
        both = u_ref[:, b, :]
        for half in range(2):
            left_ref[half * 8 + b] = jnp.concatenate(split2(both[:, half * 64:half * 64 + 64]), axis=1)

    def row_products(start, count, offset):
        def group(g, carry):
            for k in range(min(GROUP, count)):
                p = start + g * GROUP + k
                first = left_ref[rows_ref[p]]
                second = left_ref[0] if offset is None else left_ref[rows_ref[p + 128] + offset]
                c = t_ref[p].astype(BF)
                y = jnp.dot(jnp.concatenate([first, second], axis=0), jnp.concatenate([c, c], axis=0),
                            preferred_element_type=F32)
                h, l = split2(jnp.where(left, y[:64], y[64:]))
                y_ref[p] = jnp.concatenate([h, l], axis=0)
            return carry

        lax.fori_loop(0, max(1, count // GROUP), group, 0)

    def column_products(start, count, log_n, offset):
        def group(g, carry):
            for k in range(min(GROUP, count)):
                p = start + g * GROUP + k
                first = low_ref[cols_ref[p]]
                if offset is None:
                    second = high_ref[0]
                else:
                    v = cols_ref[p + 128]
                    second = high_ref[(v >> log_n) * 8 + (offset - 8) + (v & ((1 << log_n) - 1))]
                x = jnp.concatenate([first[:, :128], second[:, :128], first[:, 128:], second[:, 128:]], axis=0)
                o = dot_nt(y_ref[p], x)
                o = o[:64] + o[64:]
                o_ref[p] = o[:, :128] + o[:, 128:]
            return carry

        lax.fori_loop(0, max(1, count // GROUP), group, 0)

    for start, count, log_n, offset in PAIRS:
        row_products(start, count, offset)

    end_round(1)
    send_round(2)

    to_after.wait_recv()
    from_before = send_table(col, 3, mate, col)
    to_before.wait_recv()
    from_after = send_table(4 + col, 4, mate, 4 + col)
    to_mate.wait_recv()
    from_before.wait_recv()
    from_after.wait_recv()

    def unpack(t, carry):
        unpack_triangles(table_ref.at[t], full_ref)
        store_table(t)
        return carry

    lax.fori_loop(0, 6, unpack, 0)

    for start, count, log_n, offset in PAIRS:
        column_products(start, count, log_n, offset)

    real = valid_ref[...] == 1

    def gather(i, carry):
        x = o_ref[:, i, :].T
        x = jnp.concatenate([x[:64], x[64:, :112]], axis=1)
        out_ref[i] = jnp.where(real, x, 0.0).astype(BF)
        return carry

    lax.fori_loop(0, 64, gather, 0, unroll=4)
    store = pltpu.make_async_copy(out_ref, out_hbm, local_sem.at[1])
    store.start()

    end_round(2)
    for b in range(8):
        grams_ref[:, b, :] = jnp.concatenate([g_ref[b], g_ref[8] if b == 0 else unit], axis=1)
    store.wait()
    for copy in (to_after, to_before, to_mate, from_before, from_after):
        copy.wait_send()
    for copy in chain:
        copy.wait_send()


def path_kernel(blocks_hbm, grams_ref, out_hbm, path_ref, u_ref, blocks_ref, sem):
    fetch = pltpu.make_async_copy(blocks_hbm, blocks_ref, sem.at[0])
    store = pltpu.make_async_copy(blocks_ref, out_hbm, sem.at[1])
    fetch.start()
    factor_blocks(grams_ref, u_ref, 0, 4)
    fetch.wait()
    store.start()
    factor_blocks(grams_ref, u_ref, 4, 8)
    for k in range(9):
        path_ref[0, k] = u_ref[:, k % 8, (k // 8) * 64:(k // 8) * 64 + 64]
    store.wait()


def shards(leaf_basis, local_transfer, col_transfer, row_transfer, coupling, slot_block_row, block_col, block_valid):
    blocks = jax.ShapeDtypeStruct((64, 64, 240), BF)
    places = 1 + sum((1 << (high - low)) - 1 for low, high in ROUNDS)
    hbm = pl.BlockSpec(memory_space=pl.ANY)
    projected, grams = pl.pallas_call(
        main_kernel,
        out_shape=(blocks, jax.ShapeDtypeStruct((64, 8, 128), F32)),
        in_specs=[SMEM, SMEM, VMEM, VMEM, VMEM, VMEM, hbm, VMEM],
        out_specs=(hbm, VMEM),
        scratch_shapes=[
            pltpu.VMEM((23, 64, 192), BF),
            pltpu.VMEM((64, 8, 128), F32),
            pltpu.VMEM((64, 8, 128), F32),
            pltpu.VMEM((9, 64, 64), F32),
            pltpu.VMEM((64, 64, 240), BF),
            pltpu.VMEM((128, 64, 128), F32),
            pltpu.VMEM((128, 64, 128), F32),
            pltpu.VMEM((128, 128, 128), BF),
            pltpu.VMEM((64, 64, 240), BF),
            pltpu.VMEM((6, PACKED, 8, 128), F32),
            pltpu.VMEM((64, 8, 128), F32),
            pltpu.VMEM((16, 64, 128), BF),
            pltpu.VMEM((48, 64, 256), BF),
            pltpu.VMEM((48, 64, 256), BF),
            pltpu.VMEM((9, 32, 128), F32),
            pltpu.VMEM((places, 32, 128), F32),
            pltpu.SemaphoreType.DMA((places,)),
            pltpu.SemaphoreType.DMA((places,)),
            pltpu.SemaphoreType.DMA((5,)),
            pltpu.SemaphoreType.DMA((5,)),
            pltpu.SemaphoreType.DMA((2,)),
        ],
        compiler_params=pltpu.CompilerParams(
            vmem_limit_bytes=60 * 2**20, collective_id=0, has_side_effects=True),
        name="upsweep_and_projection",
    )(slot_block_row, block_col, leaf_basis.transpose(0, 2, 1), local_transfer, col_transfer[0], row_transfer[0],
      coupling.transpose(1, 2, 0), block_valid[None])
    projected, path_factor = pl.pallas_call(
        path_kernel,
        out_shape=(blocks, jax.ShapeDtypeStruct((1, 9, 64, 64), F32)),
        in_specs=[hbm, VMEM],
        out_specs=(hbm, VMEM),
        scratch_shapes=[
            pltpu.VMEM((64, 8, 128), F32),
            pltpu.VMEM((64, 64, 240), BF),
            pltpu.SemaphoreType.DMA((2,)),
        ],
        compiler_params=pltpu.CompilerParams(vmem_limit_bytes=60 * 2**20),
        name="path_factors",
    )(projected, grams)
    return projected.transpose(2, 0, 1), path_factor


def solution(mesh):
    placed = (
        P(("row", "col"), None, None),
        P(("row", "col"), None, None),
        P("row", None, None, None),
        P("row", None, None, None),
        P(("row", "col"), None, None),
        P(("row", "col")),
        P(("row", "col")),
        P(("row", "col")),
    )
    return jax.shard_map(
        shards,
        mesh=mesh,
        in_specs=placed,
        out_specs=(P(("row", "col"), None, None), P(("row", "col"), None, None, None)),
        check_vma=False,
    )
```

```python
import functools

import jax
import jax.numpy as jnp
from jax import lax
from jax.experimental import pallas as pl
from jax.experimental.pallas import tpu as pltpu
from jax.sharding import PartitionSpec as P

BF = jnp.bfloat16
F32 = jnp.float32
NT = (((1,), (1,)), ((), ()))
MESH = pl.DeviceIdType.MESH
VMEM = pl.BlockSpec(memory_space=pltpu.VMEM)
SMEM = pl.BlockSpec(memory_space=pltpu.SMEM)

PAIRS = ((0, 64, 2, 8), (64, 32, 1, 12), (96, 16, 0, 14), (112, 16, None, None))
ROUNDS = ((0, 2), (2, 5), (5, 8))
COL = 14
PATH = 15
GROUP = 32
PACKED = 33


def split2(x):
    high = x.astype(BF)
    return high, (x - high.astype(F32)).astype(BF)


def split3(x):
    high = x.astype(BF)
    rest = x - high.astype(F32)
    middle = rest.astype(BF)
    return high, middle, (rest - middle.astype(F32)).astype(BF)


def dot_nt(a, b):
    return lax.dot_general(a, b, NT, preferred_element_type=F32)


def gram(xt):
    h, m, l = split3(xt)
    left = jnp.concatenate([h, h, m, h, l, m], axis=1)
    right = jnp.concatenate([h, m, h, l, h, m], axis=1)
    return lax.dot_general(left, right, NT, preferred_element_type=F32)


def tripled(transfer):
    et = transfer.astype(F32).T.astype(BF)
    return jnp.concatenate([et, et, et], axis=1)


def sandwich(et3, g):
    y = lax.dot_general(et3, jnp.concatenate(split3(g), axis=1), NT, preferred_element_type=F32)
    return lax.dot_general(jnp.concatenate(split3(y), axis=1), et3, NT, preferred_element_type=F32)


def folded(g):
    return jnp.concatenate([g[:32], g[32:]], axis=1)


def unfolded(g):
    return jnp.concatenate([g[:, :64], g[:, 64:]], axis=0)


def take(row, index):
    return jnp.take_along_axis(row, index, axis=1, mode="promise_in_bounds")


def factor_blocks(a_ref, u_ref, low, high, beside=None, before=None, after=None):
    lane = lax.broadcasted_iota(jnp.int32, (8, 128), 1)
    half = lane // 64 * 64
    column = lane % 64

    def block(number, carry):
        if before is not None:
            before(number)
        first = number * 8
        index = [half + (first + i) for i in range(8)]

        def update(g, rows):
            done = [u_ref[g * 8 + m] for m in range(8)]
            fresh = []
            for i in range(8):
                terms = [take(done[m], index[i]) * done[m] for m in range(8)]
                while len(terms) > 1:
                    terms = [terms[k] + terms[k + 1] for k in range(0, len(terms), 2)]
                fresh.append(rows[i] - terms[0])
            return tuple(fresh)

        rows = list(lax.fori_loop(0, number, update, tuple(a_ref[first + i] for i in range(8))))
        if beside is not None:
            beside(number)
        entry = {}
        for j in range(8):
            for i in range(j + 1):
                entry[i, j] = take(rows[i], index[j])
        for k in range(8):
            scale = lax.rsqrt(entry[k, k])
            top = rows[k] * scale
            u_ref[first + k] = jnp.where(column < first + k, 0.0, top)
            factor = {j: entry[k, j] * scale for j in range(k + 1, 8)}
            for i in range(k + 1, 8):
                rows[i] = rows[i] - factor[i] * top
                for j in range(i, 8):
                    entry[i, j] = entry[i, j] - factor[i] * factor[j]
        if after is not None:
            after(number)
        return carry

    lax.fori_loop(low, high, block, 0)


def partners(row, rounds):
    found = []
    for low, high in rounds:
        for d in range(1, 1 << (high - low)):
            block = 1 << low
            digit = row // block % (1 << (high - low))
            flipped = 0
            for bit in range(high - low):
                own = digit // (1 << bit) % 2
                flipped = flipped + ((1 - own) if d >> bit & 1 else own) * (1 << bit)
            found.append(row + (flipped - digit) * block)
    return found


def local_grams(leaf_ref, et_ref):
    level = [gram(leaf_ref[i]) for i in range(8)]
    grams = list(level)
    offset = 0
    while len(level) > 1:
        parts = [sandwich(et_ref[offset + i], g) for i, g in enumerate(level)]
        offset += len(level)
        level = [parts[i] + parts[i + 1] for i in range(0, len(parts), 2)]
        grams += level
    return grams


def pack_triangles(u_ref, packed_ref):
    column = lax.broadcasted_iota(jnp.int32, (8, 128), 1) % 64
    packed_ref[0] = u_ref[0]
    packed_ref[32] = u_ref[32]
    for i in range(1, 32):
        packed_ref[i] = jnp.where(column >= i, u_ref[i], pltpu.roll(u_ref[64 - i], i, 1))


def unpack_triangles(packed_ref, u_ref):
    column = lax.broadcasted_iota(jnp.int32, (8, 128), 1) % 64
    u_ref[0] = packed_ref[0]
    u_ref[32] = packed_ref[32]
    for i in range(1, 32):
        both = packed_ref[i]
        u_ref[i] = jnp.where(column >= i, both, 0.0)
        u_ref[64 - i] = pltpu.roll(jnp.where(column >= i, 0.0, both), 128 - i, 1)


def main_kernel(rows_ref, cols_ref, leaf_ref, local_ref, col_ref, path_ref, ct_hbm, out_hbm, grams_ref,
                et_ref, a_ref, u_ref, g_ref, ct_ref, t_ref, o_ref, y_ref, table_ref, full_ref, left_ref, low_ref,
                high_ref, out_buf, in_buf, send_sem, recv_sem, tab_send, tab_recv, local_sem):
    row = lax.axis_index("row")
    col = lax.axis_index("col")
    rows = lax.axis_size("row")
    after = lax.rem(row + 1, rows)
    before = lax.rem(row + rows - 1, rows)
    others = partners(row, ROUNDS)
    mate = (row, 1 - col)
    left = lax.broadcasted_iota(jnp.int32, (64, 128), 1) < 64

    fetch = pltpu.make_async_copy(ct_hbm, ct_ref, local_sem.at[0])
    fetch.start()
    barrier = pltpu.get_barrier_semaphore()
    for device in [mate, (before, col), (after, col)] + [(r, col) for r in others]:
        pl.semaphore_signal(barrier, inc=1, device_id=device, device_id_type=MESH)

    def send(slot, target, place):
        copy = pltpu.make_async_remote_copy(
            src_ref=out_buf.at[slot], dst_ref=in_buf.at[place],
            send_sem=send_sem.at[place], recv_sem=recv_sem.at[place],
            device_id=target, device_id_type=MESH)
        copy.start()
        return copy

    def send_table(place, sem, target, there):
        copy = pltpu.make_async_remote_copy(
            src_ref=table_ref.at[place], dst_ref=table_ref.at[there],
            send_sem=tab_send.at[sem], recv_sem=tab_recv.at[sem],
            device_id=target, device_id_type=MESH)
        copy.start()
        return copy

    chain = []
    starts = []
    for low, high in ROUNDS:
        starts.append((1 + sum((1 << (b - a)) - 1 for a, b in ROUNDS if a < low), low, high))

    def send_round(number):
        first, low, high = starts[number]
        own = g_ref[low]
        place = first
        for t in range(1, high - low + 1):
            own = sandwich(et_ref[PATH + low + t - 1], own)
            out_buf[low + t] = folded(own)
            for d in range(1 << (t - 1), 1 << t):
                chain.append(send(low + t, (others[place - 1], col), place))
                place += 1

    def end_round(number):
        first, low, high = starts[number]
        place = first
        for t in range(1, high - low + 1):
            if t == 1:
                total = out_buf[low + 1]
            else:
                total = folded(sandwich(et_ref[PATH + low + t - 1], g_ref[low + t - 1]))
            for d in range(1 << (t - 1), 1 << t):
                chain[place].wait_recv()
                total = total + in_buf[place]
                place += 1
            g_ref[low + t] = unfolded(total)

    def store_table(t, source):
        for b in range(8):
            x = source[:, b, :]
            low_ref[t * 8 + b] = jnp.concatenate(split2(jnp.where(left, x, 0.0)), axis=1)
            high_ref[t * 8 + b] = jnp.concatenate(split2(jnp.where(left, 0.0, x)), axis=1)

    for i in range(14):
        et_ref[i] = tripled(local_ref[i])
    et_ref[COL] = tripled(col_ref[col])
    grams = local_grams(leaf_ref, et_ref)
    out_buf[0] = folded(sandwich(et_ref[COL], grams[14]))
    pl.semaphore_wait(barrier, 3 + len(others))
    chain.append(send(0, mate, 0))

    unit = jnp.where(lax.broadcasted_iota(jnp.int32, (64, 64), 0)
                     == lax.broadcasted_iota(jnp.int32, (64, 64), 1), 1.0, 0.0)
    grams.append(unit)
    for b in range(8):
        a_ref[:, b, :] = jnp.concatenate([grams[b], grams[8 + b]], axis=1)
    for k in range(8):
        et_ref[PATH + k] = tripled(path_ref[k])

    fetch.wait()
    pad = jnp.zeros((64, 16), F32)

    def spread(number):
        for k in range(8):
            x = ct_ref[number * 8 + k].astype(F32)
            later = jnp.concatenate([x[:, 128:], pad], axis=1)
            t_ref[:, number * 8 + k, :] = jnp.concatenate([x[:, :128], later], axis=0).T

    factor_blocks(a_ref, u_ref, 0, 3, spread)
    chain[0].wait_recv()
    g_ref[0] = unfolded(out_buf[0] + in_buf[0])
    send_round(0)
    factor_blocks(a_ref, u_ref, 3, 8, spread)
    mine = 2 + col
    pack_triangles(u_ref, table_ref.at[mine])
    to_after = send_table(mine, 0, (after, col), col)
    to_before = send_table(mine, 1, (before, col), 4 + col)
    to_mate = send_table(mine, 2, mate, mine)
    end_round(0)
    send_round(1)

    def row_products(start, count, offset):
        def group(g, carry):
            for k in range(min(GROUP, count)):
                p = start + g * GROUP + k
                first = left_ref[rows_ref[p]]
                second = left_ref[0] if offset is None else left_ref[rows_ref[p + 128] + offset]
                c = t_ref[p].astype(BF)
                y = jnp.dot(jnp.concatenate([first, second], axis=0), jnp.concatenate([c, c], axis=0),
                            preferred_element_type=F32)
                h, l = split2(jnp.where(left, y[:64], y[64:]))
                y_ref[p] = jnp.concatenate([h, l], axis=0)
            return carry

        lax.fori_loop(0, max(1, count // GROUP), group, 0)

    def column_products(start, count, log_n, offset):
        def group(g, carry):
            for k in range(min(GROUP, count)):
                p = start + g * GROUP + k
                first = low_ref[cols_ref[p]]
                if offset is None:
                    second = high_ref[0]
                else:
                    v = cols_ref[p + 128]
                    second = high_ref[(v >> log_n) * 8 + (offset - 8) + (v & ((1 << log_n) - 1))]
                x = jnp.concatenate([first[:, :128], second[:, :128], first[:, 128:], second[:, 128:]], axis=0)
                o = dot_nt(y_ref[p], x)
                o = o[:64] + o[64:]
                o_ref[:, p, :] = o[:, :128] + o[:, 128:]
            return carry

        lax.fori_loop(0, max(1, count // GROUP), group, 0)

    for b in range(8):
        both = u_ref[:, b, :]
        for half in range(2):
            left_ref[half * 8 + b] = jnp.concatenate(split2(both[:, half * 64:half * 64 + 64]), axis=1)

    store_table(mine, u_ref)
    for start, count, log_n, offset in PAIRS:
        row_products(start, count, offset)

    end_round(1)
    send_round(2)

    def open_table(t):
        unpack_triangles(table_ref.at[t], full_ref)
        store_table(t, full_ref)

    to_mate.wait_recv()
    open_table(3 - col)
    to_before.wait_recv()
    from_after = send_table(4 + col, 4, mate, 4 + col)
    open_table(4 + col)
    to_after.wait_recv()
    from_before = send_table(col, 3, mate, col)
    open_table(col)
    from_after.wait_recv()
    open_table(5 - col)
    from_before.wait_recv()
    open_table(1 - col)

    stores = []
    for number, (start, count, log_n, offset) in enumerate(PAIRS):
        column_products(start, count, log_n, offset)
        part = pl.ds(start, count)
        stores.append(pltpu.make_async_copy(o_ref.at[:, part], out_hbm.at[:, part], local_sem.at[1 + number]))
        stores[-1].start()

    end_round(2)
    for b in range(8):
        grams_ref[:, b, :] = jnp.concatenate([g_ref[b], g_ref[8] if b == 0 else unit], axis=1)
    for copy in stores:
        copy.wait()
    for copy in (to_after, to_before, to_mate, from_before, from_after):
        copy.wait_send()
    for copy in chain:
        copy.wait_send()


def path_kernel(valid_hbm, products_hbm, grams_hbm, out_hbm, path_ref, valid_ref, grams_ref, u_ref, products_ref,
                out_ref, first_sem, fetch_sem, store_sem):
    first = (pltpu.make_async_copy(grams_hbm, grams_ref, first_sem.at[0]),
             pltpu.make_async_copy(valid_hbm, valid_ref, first_sem.at[1]))
    for copy in first:
        copy.start()

    def fetch(number):
        rows = pl.ds(pl.multiple_of(number * 8, 8), 8)
        return pltpu.make_async_copy(products_hbm.at[rows], products_ref.at[rows], fetch_sem.at[number])

    def store(number):
        rows = pl.ds(number * 8, 8)
        return pltpu.make_async_copy(out_ref.at[rows], out_hbm.at[rows], store_sem.at[number])

    def gather(number):
        for k in range(8):
            x = products_ref[number * 8 + k].T
            x = jnp.concatenate([x[:64], x[64:, :112]], axis=1)
            out_ref[number * 8 + k] = jnp.where(real, x, 0.0).astype(BF)

    for number in range(8):
        fetch(number).start()
    for copy in first:
        copy.wait()
    real = valid_ref[...] == 1
    factor_blocks(grams_ref, u_ref, 0, 8, gather,
                  before=lambda number: fetch(number).wait(), after=lambda number: store(number).start())
    for k in range(9):
        path_ref[0, k] = u_ref[:, k % 8, (k // 8) * 64:(k // 8) * 64 + 64]
    for number in range(8):
        store(number).wait()


def shards(leaf_basis, local_transfer, col_transfer, row_transfer, coupling, slot_block_row, block_col, block_valid):
    blocks = jax.ShapeDtypeStruct((64, 64, 240), BF)
    places = 1 + sum((1 << (high - low)) - 1 for low, high in ROUNDS)
    hbm = pl.BlockSpec(memory_space=pl.ANY)
    products, grams = pl.pallas_call(
        main_kernel,
        out_shape=(jax.ShapeDtypeStruct((64, 128, 128), F32), jax.ShapeDtypeStruct((64, 8, 128), F32)),
        in_specs=[SMEM, SMEM, VMEM, VMEM, VMEM, VMEM, hbm],
        out_specs=(hbm, VMEM),
        scratch_shapes=[
            pltpu.VMEM((23, 64, 192), BF),
            pltpu.VMEM((64, 8, 128), F32),
            pltpu.VMEM((64, 8, 128), F32),
            pltpu.VMEM((9, 64, 64), F32),
            pltpu.VMEM((64, 64, 240), BF),
            pltpu.VMEM((128, 64, 128), F32),
            pltpu.VMEM((64, 128, 128), F32),
            pltpu.VMEM((128, 128, 128), BF),
            pltpu.VMEM((6, PACKED, 8, 128), F32),
            pltpu.VMEM((64, 8, 128), F32),
            pltpu.VMEM((16, 64, 128), BF),
            pltpu.VMEM((48, 64, 256), BF),
            pltpu.VMEM((48, 64, 256), BF),
            pltpu.VMEM((9, 32, 128), F32),
            pltpu.VMEM((places, 32, 128), F32),
            pltpu.SemaphoreType.DMA((places,)),
            pltpu.SemaphoreType.DMA((places,)),
            pltpu.SemaphoreType.DMA((5,)),
            pltpu.SemaphoreType.DMA((5,)),
            pltpu.SemaphoreType.DMA((5,)),
        ],
        compiler_params=pltpu.CompilerParams(
            vmem_limit_bytes=60 * 2**20, collective_id=0, has_side_effects=True),
        name="upsweep_and_projection",
    )(slot_block_row, block_col, leaf_basis.transpose(0, 2, 1), local_transfer, col_transfer[0], row_transfer[0],
      coupling.transpose(1, 2, 0))
    projected, path_factor = pl.pallas_call(
        path_kernel,
        out_shape=(blocks, jax.ShapeDtypeStruct((1, 9, 64, 64), F32)),
        in_specs=[hbm] * 3,
        out_specs=(hbm, VMEM),
        scratch_shapes=[
            pltpu.VMEM((1, 240), jnp.int32),
            pltpu.VMEM((64, 8, 128), F32),
            pltpu.VMEM((64, 8, 128), F32),
            pltpu.VMEM((64, 128, 128), F32),
            pltpu.VMEM((64, 64, 240), BF),
            pltpu.SemaphoreType.DMA((2,)),
            pltpu.SemaphoreType.DMA((8,)),
            pltpu.SemaphoreType.DMA((8,)),
        ],
        compiler_params=pltpu.CompilerParams(vmem_limit_bytes=60 * 2**20),
        name="path_factors",
    )(block_valid[None], products, grams)
    return projected.transpose(2, 0, 1), path_factor


def solution(mesh):
    placed = (
        P(("row", "col"), None, None),
        P(("row", "col"), None, None),
        P("row", None, None, None),
        P("row", None, None, None),
        P(("row", "col"), None, None),
        P(("row", "col")),
        P(("row", "col")),
        P(("row", "col")),
    )
    return jax.shard_map(
        shards,
        mesh=mesh,
        in_specs=placed,
        out_specs=(P(("row", "col"), None, None), P(("row", "col"), None, None, None)),
        check_vma=False,
    )
```

```python
import functools

import jax
import jax.numpy as jnp
from jax import lax
from jax.experimental import pallas as pl
from jax.experimental.pallas import tpu as pltpu
from jax.sharding import PartitionSpec as P

BF = jnp.bfloat16
F32 = jnp.float32
NT = (((1,), (1,)), ((), ()))
MESH = pl.DeviceIdType.MESH
VMEM = pl.BlockSpec(memory_space=pltpu.VMEM)
SMEM = pl.BlockSpec(memory_space=pltpu.SMEM)

PAIRS = ((0, 64, 2, 8), (64, 32, 1, 12), (96, 16, 0, 14), (112, 16, None, None))
ROUNDS = ((0, 2), (2, 5), (5, 8))
COL = 14
PATH = 15
GROUP = 32
PACKED = 33


def split2(x):
    high = x.astype(BF)
    return high, (x - high.astype(F32)).astype(BF)


def split3(x):
    high = x.astype(BF)
    rest = x - high.astype(F32)
    middle = rest.astype(BF)
    return high, middle, (rest - middle.astype(F32)).astype(BF)


def dot_nt(a, b):
    return lax.dot_general(a, b, NT, preferred_element_type=F32)


def gram(xt):
    h, m, l = split3(xt)
    left = jnp.concatenate([h, h, m, h, l, m], axis=1)
    right = jnp.concatenate([h, m, h, l, h, m], axis=1)
    return lax.dot_general(left, right, NT, preferred_element_type=F32)


def tripled(transfer):
    et = transfer.astype(F32).T.astype(BF)
    return jnp.concatenate([et, et, et], axis=1)


def sandwich(et3, g):
    y = lax.dot_general(et3, jnp.concatenate(split3(g), axis=1), NT, preferred_element_type=F32)
    return lax.dot_general(jnp.concatenate(split3(y), axis=1), et3, NT, preferred_element_type=F32)


def folded(g):
    return jnp.concatenate([g[:32], g[32:]], axis=1)


def unfolded(g):
    return jnp.concatenate([g[:, :64], g[:, 64:]], axis=0)


def take(row, index):
    return jnp.take_along_axis(row, index, axis=1, mode="promise_in_bounds")


def factor_blocks(a_ref, u_ref, low, high, beside=None, before=None, after=None):
    lane = lax.broadcasted_iota(jnp.int32, (8, 128), 1)
    half = lane // 64 * 64
    column = lane % 64

    def block(number, carry):
        if before is not None:
            before(number)
        first = number * 8
        index = [half + (first + i) for i in range(8)]

        def update(g, rows):
            done = [u_ref[g * 8 + m] for m in range(8)]
            fresh = []
            for i in range(8):
                terms = [take(done[m], index[i]) * done[m] for m in range(8)]
                while len(terms) > 1:
                    terms = [terms[k] + terms[k + 1] for k in range(0, len(terms), 2)]
                fresh.append(rows[i] - terms[0])
            return tuple(fresh)

        rows = list(lax.fori_loop(0, number, update, tuple(a_ref[first + i] for i in range(8))))
        if beside is not None:
            beside(number)
        entry = {}
        for j in range(8):
            for i in range(j + 1):
                entry[i, j] = take(rows[i], index[j])
        for k in range(8):
            scale = lax.rsqrt(entry[k, k])
            top = rows[k] * scale
            u_ref[first + k] = jnp.where(column < first + k, 0.0, top)
            factor = {j: entry[k, j] * scale for j in range(k + 1, 8)}
            for i in range(k + 1, 8):
                rows[i] = rows[i] - factor[i] * top
                for j in range(i, 8):
                    entry[i, j] = entry[i, j] - factor[i] * factor[j]
        if after is not None:
            after(number)
        return carry

    lax.fori_loop(low, high, block, 0)


def partners(row, rounds):
    found = []
    for low, high in rounds:
        for d in range(1, 1 << (high - low)):
            block = 1 << low
            digit = row // block % (1 << (high - low))
            flipped = 0
            for bit in range(high - low):
                own = digit // (1 << bit) % 2
                flipped = flipped + ((1 - own) if d >> bit & 1 else own) * (1 << bit)
            found.append(row + (flipped - digit) * block)
    return found


def local_grams(leaf_ref, et_ref):
    level = [gram(leaf_ref[i]) for i in range(8)]
    grams = list(level)
    offset = 0
    while len(level) > 1:
        parts = [sandwich(et_ref[offset + i], g) for i, g in enumerate(level)]
        offset += len(level)
        level = [parts[i] + parts[i + 1] for i in range(0, len(parts), 2)]
        grams += level
    return grams


def pack_triangles(u_ref, packed_ref):
    column = lax.broadcasted_iota(jnp.int32, (8, 128), 1) % 64
    packed_ref[0] = u_ref[0]
    packed_ref[32] = u_ref[32]
    for i in range(1, 32):
        packed_ref[i] = jnp.where(column >= i, u_ref[i], pltpu.roll(u_ref[64 - i], i, 1))


def unpack_triangles(packed_ref, u_ref):
    column = lax.broadcasted_iota(jnp.int32, (8, 128), 1) % 64
    u_ref[0] = packed_ref[0]
    u_ref[32] = packed_ref[32]
    for i in range(1, 32):
        both = packed_ref[i]
        u_ref[i] = jnp.where(column >= i, both, 0.0)
        u_ref[64 - i] = pltpu.roll(jnp.where(column >= i, 0.0, both), 128 - i, 1)


def main_kernel(rows_ref, cols_ref, leaf_ref, local_ref, col_ref, path_ref, ct_hbm, out_hbm, grams_ref,
                et_ref, a_ref, u_ref, g_ref, ct_ref, t_ref, o_ref, y_ref, table_ref, full_ref, left_ref, low_ref,
                high_ref, out_buf, in_buf, send_sem, recv_sem, tab_send, tab_recv, local_sem):
    row = lax.axis_index("row")
    col = lax.axis_index("col")
    rows = lax.axis_size("row")
    after = lax.rem(row + 1, rows)
    before = lax.rem(row + rows - 1, rows)
    others = partners(row, ROUNDS)
    mate = (row, 1 - col)
    left = lax.broadcasted_iota(jnp.int32, (64, 128), 1) < 64

    fetch = pltpu.make_async_copy(ct_hbm, ct_ref, local_sem.at[0])
    fetch.start()
    barrier = pltpu.get_barrier_semaphore()
    for device in [mate, (before, col), (after, col)] + [(r, col) for r in others]:
        pl.semaphore_signal(barrier, inc=1, device_id=device, device_id_type=MESH)

    def send(slot, target, place):
        copy = pltpu.make_async_remote_copy(
            src_ref=out_buf.at[slot], dst_ref=in_buf.at[place],
            send_sem=send_sem.at[place], recv_sem=recv_sem.at[place],
            device_id=target, device_id_type=MESH)
        copy.start()
        return copy

    def send_table(place, sem, target, there):
        copy = pltpu.make_async_remote_copy(
            src_ref=table_ref.at[place], dst_ref=table_ref.at[there],
            send_sem=tab_send.at[sem], recv_sem=tab_recv.at[sem],
            device_id=target, device_id_type=MESH)
        copy.start()
        return copy

    chain = []
    starts = []
    for low, high in ROUNDS:
        starts.append((1 + sum((1 << (b - a)) - 1 for a, b in ROUNDS if a < low), low, high))

    def send_round(number):
        first, low, high = starts[number]
        own = g_ref[low]
        place = first
        for t in range(1, high - low + 1):
            own = sandwich(et_ref[PATH + low + t - 1], own)
            out_buf[low + t] = folded(own)
            for d in range(1 << (t - 1), 1 << t):
                chain.append(send(low + t, (others[place - 1], col), place))
                place += 1

    def end_round(number):
        first, low, high = starts[number]
        place = first
        for t in range(1, high - low + 1):
            if t == 1:
                total = out_buf[low + 1]
            else:
                total = folded(sandwich(et_ref[PATH + low + t - 1], g_ref[low + t - 1]))
            for d in range(1 << (t - 1), 1 << t):
                chain[place].wait_recv()
                total = total + in_buf[place]
                place += 1
            g_ref[low + t] = unfolded(total)

    def store_table(t, source):
        for b in range(8):
            x = source[:, b, :]
            low_ref[t * 8 + b] = jnp.concatenate(split2(jnp.where(left, x, 0.0)), axis=1)
            high_ref[t * 8 + b] = jnp.concatenate(split2(jnp.where(left, 0.0, x)), axis=1)

    for i in range(14):
        et_ref[i] = tripled(local_ref[i])
    et_ref[COL] = tripled(col_ref[col])
    grams = local_grams(leaf_ref, et_ref)
    out_buf[0] = folded(sandwich(et_ref[COL], grams[14]))
    pl.semaphore_wait(barrier, 3 + len(others))
    chain.append(send(0, mate, 0))

    unit = jnp.where(lax.broadcasted_iota(jnp.int32, (64, 64), 0)
                     == lax.broadcasted_iota(jnp.int32, (64, 64), 1), 1.0, 0.0)
    grams.append(unit)
    for b in range(8):
        a_ref[:, b, :] = jnp.concatenate([grams[b], grams[8 + b]], axis=1)
    for k in range(8):
        et_ref[PATH + k] = tripled(path_ref[k])

    fetch.wait()
    pad = jnp.zeros((64, 16), F32)

    def spread(number):
        for k in range(8):
            x = ct_ref[number * 8 + k].astype(F32)
            later = jnp.concatenate([x[:, 128:], pad], axis=1)
            t_ref[:, number * 8 + k, :] = jnp.concatenate([x[:, :128], later], axis=0).T

    factor_blocks(a_ref, u_ref, 0, 2, spread)
    chain[0].wait_recv()
    g_ref[0] = unfolded(out_buf[0] + in_buf[0])
    send_round(0)
    factor_blocks(a_ref, u_ref, 2, 8, spread)
    mine = 2 + col
    pack_triangles(u_ref, table_ref.at[mine])
    to_after = send_table(mine, 0, (after, col), col)
    to_before = send_table(mine, 1, (before, col), 4 + col)
    to_mate = send_table(mine, 2, mate, mine)
    end_round(0)
    send_round(1)

    def row_products(start, count, offset):
        def group(g, carry):
            for k in range(min(GROUP, count)):
                p = start + g * GROUP + k
                first = left_ref[rows_ref[p]]
                second = left_ref[0] if offset is None else left_ref[rows_ref[p + 128] + offset]
                c = t_ref[p].astype(BF)
                y = jnp.dot(jnp.concatenate([first, second], axis=0), jnp.concatenate([c, c], axis=0),
                            preferred_element_type=F32)
                h, l = split2(jnp.where(left, y[:64], y[64:]))
                y_ref[p] = jnp.concatenate([h, l], axis=0)
            return carry

        lax.fori_loop(0, max(1, count // GROUP), group, 0)

    def column_products(start, count, log_n, offset):
        def group(g, carry):
            for k in range(min(GROUP, count)):
                p = start + g * GROUP + k
                first = low_ref[cols_ref[p]]
                if offset is None:
                    second = high_ref[0]
                else:
                    v = cols_ref[p + 128]
                    second = high_ref[(v >> log_n) * 8 + (offset - 8) + (v & ((1 << log_n) - 1))]
                x = jnp.concatenate([first[:, :128], second[:, :128], first[:, 128:], second[:, 128:]], axis=0)
                o = dot_nt(y_ref[p], x)
                o = o[:64] + o[64:]
                o_ref[:, p, :] = o[:, :128] + o[:, 128:]
            return carry

        lax.fori_loop(0, max(1, count // GROUP), group, 0)

    for b in range(8):
        both = u_ref[:, b, :]
        for half in range(2):
            left_ref[half * 8 + b] = jnp.concatenate(split2(both[:, half * 64:half * 64 + 64]), axis=1)

    store_table(mine, u_ref)
    for start, count, log_n, offset in PAIRS:
        row_products(start, count, offset)

    end_round(1)
    send_round(2)

    def open_table(t):
        unpack_triangles(table_ref.at[t], full_ref)
        store_table(t, full_ref)

    to_mate.wait_recv()
    open_table(3 - col)
    to_before.wait_recv()
    from_after = send_table(4 + col, 4, mate, 4 + col)
    open_table(4 + col)
    to_after.wait_recv()
    from_before = send_table(col, 3, mate, col)
    open_table(col)
    from_after.wait_recv()
    open_table(5 - col)
    from_before.wait_recv()
    open_table(1 - col)

    stores = []
    for number, (start, count, log_n, offset) in enumerate(PAIRS):
        column_products(start, count, log_n, offset)
        part = pl.ds(start, count)
        stores.append(pltpu.make_async_copy(o_ref.at[:, part], out_hbm.at[:, part], local_sem.at[1 + number]))
        stores[-1].start()

    end_round(2)
    for b in range(8):
        grams_ref[:, b, :] = jnp.concatenate([g_ref[b], g_ref[8] if b == 0 else unit], axis=1)
    for copy in stores:
        copy.wait()
    for copy in (to_after, to_before, to_mate, from_before, from_after):
        copy.wait_send()
    for copy in chain:
        copy.wait_send()


def path_kernel(valid_hbm, products_hbm, grams_hbm, out_hbm, path_ref, valid_ref, grams_ref, u_ref, products_ref,
                out_ref, first_sem, fetch_sem, store_sem):
    first = (pltpu.make_async_copy(grams_hbm, grams_ref, first_sem.at[0]),
             pltpu.make_async_copy(valid_hbm, valid_ref, first_sem.at[1]))
    for copy in first:
        copy.start()

    def fetch(number):
        rows = pl.ds(pl.multiple_of(number * 8, 8), 8)
        return pltpu.make_async_copy(products_hbm.at[rows], products_ref.at[rows], fetch_sem.at[number])

    def store(number):
        rows = pl.ds(number * 8, 8)
        return pltpu.make_async_copy(out_ref.at[rows], out_hbm.at[rows], store_sem.at[number])

    def gather(number):
        for k in range(8):
            x = products_ref[number * 8 + k].T
            x = jnp.concatenate([x[:64], x[64:, :112]], axis=1)
            out_ref[number * 8 + k] = jnp.where(real, x, 0.0).astype(BF)

    for number in range(8):
        fetch(number).start()
    for copy in first:
        copy.wait()
    real = valid_ref[...] == 1
    factor_blocks(grams_ref, u_ref, 0, 8, gather,
                  before=lambda number: fetch(number).wait(), after=lambda number: store(number).start())
    for k in range(9):
        path_ref[0, k] = u_ref[:, k % 8, (k // 8) * 64:(k // 8) * 64 + 64]
    for number in range(8):
        store(number).wait()


def shards(leaf_basis, local_transfer, col_transfer, row_transfer, coupling, slot_block_row, block_col, block_valid):
    blocks = jax.ShapeDtypeStruct((64, 64, 240), BF)
    places = 1 + sum((1 << (high - low)) - 1 for low, high in ROUNDS)
    hbm = pl.BlockSpec(memory_space=pl.ANY)
    products, grams = pl.pallas_call(
        main_kernel,
        out_shape=(jax.ShapeDtypeStruct((64, 128, 128), F32), jax.ShapeDtypeStruct((64, 8, 128), F32)),
        in_specs=[SMEM, SMEM, VMEM, VMEM, VMEM, VMEM, hbm],
        out_specs=(hbm, VMEM),
        scratch_shapes=[
            pltpu.VMEM((23, 64, 192), BF),
            pltpu.VMEM((64, 8, 128), F32),
            pltpu.VMEM((64, 8, 128), F32),
            pltpu.VMEM((9, 64, 64), F32),
            pltpu.VMEM((64, 64, 240), BF),
            pltpu.VMEM((128, 64, 128), F32),
            pltpu.VMEM((64, 128, 128), F32),
            pltpu.VMEM((128, 128, 128), BF),
            pltpu.VMEM((6, PACKED, 8, 128), F32),
            pltpu.VMEM((64, 8, 128), F32),
            pltpu.VMEM((16, 64, 128), BF),
            pltpu.VMEM((48, 64, 256), BF),
            pltpu.VMEM((48, 64, 256), BF),
            pltpu.VMEM((9, 32, 128), F32),
            pltpu.VMEM((places, 32, 128), F32),
            pltpu.SemaphoreType.DMA((places,)),
            pltpu.SemaphoreType.DMA((places,)),
            pltpu.SemaphoreType.DMA((5,)),
            pltpu.SemaphoreType.DMA((5,)),
            pltpu.SemaphoreType.DMA((5,)),
        ],
        compiler_params=pltpu.CompilerParams(
            vmem_limit_bytes=60 * 2**20, collective_id=0, has_side_effects=True),
        name="upsweep_and_projection",
    )(slot_block_row, block_col, leaf_basis.transpose(0, 2, 1), local_transfer, col_transfer[0], row_transfer[0],
      coupling.transpose(1, 2, 0))
    projected, path_factor = pl.pallas_call(
        path_kernel,
        out_shape=(blocks, jax.ShapeDtypeStruct((1, 9, 64, 64), F32)),
        in_specs=[hbm] * 3,
        out_specs=(hbm, VMEM),
        scratch_shapes=[
            pltpu.VMEM((1, 240), jnp.int32),
            pltpu.VMEM((64, 8, 128), F32),
            pltpu.VMEM((64, 8, 128), F32),
            pltpu.VMEM((64, 128, 128), F32),
            pltpu.VMEM((64, 64, 240), BF),
            pltpu.SemaphoreType.DMA((2,)),
            pltpu.SemaphoreType.DMA((8,)),
            pltpu.SemaphoreType.DMA((8,)),
        ],
        compiler_params=pltpu.CompilerParams(vmem_limit_bytes=60 * 2**20),
        name="path_factors",
    )(block_valid[None], products, grams)
    return projected.transpose(2, 0, 1), path_factor


def solution(mesh):
    placed = (
        P(("row", "col"), None, None),
        P(("row", "col"), None, None),
        P("row", None, None, None),
        P("row", None, None, None),
        P(("row", "col"), None, None),
        P(("row", "col")),
        P(("row", "col")),
        P(("row", "col")),
    )
    return jax.shard_map(
        shards,
        mesh=mesh,
        in_specs=placed,
        out_specs=(P(("row", "col"), None, None), P(("row", "col"), None, None, None)),
        check_vma=False,
    )
```
